1024 devices in a mesh: fsdp: 32 (over z), dp: 4 (over y), mp: 8 (over x, core).
Axes of the slice: x: 4, y: 4, z: 32, core: 2. Of those that a mesh axis runs over, the one named last changes fastest.
Arguments:
- grad_parts: bfloat16 [4, 1024, 256, 256], P('dp', 'mp', 'fsdp'), may hold values from -6 to 6
- owner_ids: int32 [1024, 1], P('mp'), may hold values from 0 to 31; in each aligned block of 32 rows (0 to 31, 32 to 63, ...) at most 2 rows name the same one
- factors: float32 [8, 4, 64, 2, 256, 256], P('mp', 'dp', 'fsdp'), as said below
Outputs:
- directions: bfloat16 [1024, 256, 256], P('mp', 'fsdp')
- new_factors: float32 [8, 4, 64, 2, 256, 256], P('mp', 'dp', 'fsdp')
The draws below stay inside these ranges and needn't reach their ends.
Inputs may be any that keep to these rules, and one draw needn't show every extreme that they name: `owner_ids`: in each aligned block of 32 rows (the blocks of one group) no owner is named more than 2 times, a bound that some block reaches. `factors`: every factor is symmetric and each diagonal entry exceeds the sum of magnitudes of the other entries of its row.
All inputs are finite; a program needn't handle non-finite values. Where the reference program divides by a largest or mean magnitude, that divisor is 1e-20 or more.
Results may differ from the reference program's by a relative error of at most 0.015.
Values may be sent and summed in bfloat16 or wider, within the bound.
No kernel may reach another device: no remote copies, remote signals or barrier semaphores. Data moves between devices by JAX's collectives and lax.ppermute only.
A program may use at most 32 MiB of HBM per device.

```python
import math
import jax
import jax.numpy as jnp
import numpy as np
from jax import lax

BLK = 256
CAP = 2
NBD = 32
NB = 1024
N_FSDP = 32
N_DP = 4
N_MP = 8


def draw_factors(key, part):
    key = jax.random.fold_in(key, 7)
    full_shape = (N_MP, N_DP, N_FSDP * CAP, 2, BLK, BLK)
    noise_key, level_key = jax.random.split(key)
    raw_noise = jax.random.uniform(noise_key, full_shape, jnp.float32, -2.0, 2.0)
    symmetric = 0.5 * (raw_noise + jnp.swapaxes(raw_noise, -1, -2))
    diag_level = jax.random.uniform(level_key, full_shape[:-1], jnp.float32, 1.1, 3.0)
    identity = jnp.eye(BLK, dtype=jnp.float32)
    diagonal = diag_level * (2.0 * (BLK - 1))
    return symmetric * (1.0 - identity) + identity * diagonal[..., None]


def block_scale(stream_key, extent, pieces, smallest, high):
    loudness = 1.0
    for position, shards_of in pieces:
        heights = jax.random.uniform(jax.random.fold_in(jax.random.fold_in(stream_key, 6), position), (shards_of,), jnp.float32, smallest / len(pieces), high / len(pieces))
        loudness = loudness * jnp.repeat(jnp.exp(heights), extent[position] // shards_of).reshape((-1,) + (1,) * (len(extent) - 1 - position))
    return loudness


def shared_out(rng, own, number, rows, amount, top, most, slope):
    ranking = jax.random.permutation(rng, amount)
    packed, common = portions_of(amount, rows * top, most, slope, True), portions_of(amount, rows * top, most, slope, False)
    places = jnp.arange(amount)

    def named(tallies, offset_by):
        used = int((tallies > 0).sum())
        fixed = max(1, used // 4)
        moved = fixed + (places - fixed + offset_by * (used - fixed)) % max(1, amount - fixed)
        return jnp.zeros((amount,), jnp.int32).at[ranking[jnp.where(places < fixed, places, moved)]].set(jnp.asarray(tallies, jnp.int32))

    tallies = jnp.where(number % 4 == 0, named(packed, number // 4), named(common, number - number // 4 - 1))
    mixed = jax.random.permutation(jax.random.fold_in(own, 3), amount)
    source_of, taker = mixed[0:amount // 2 * 2:2], mixed[1:amount // 2 * 2:2]
    room = jnp.minimum(tallies[source_of] - 1, most - tallies[taker]) // 2
    room = jnp.where((source_of == ranking[0]) | (taker == ranking[0]) | (tallies[taker] == 0), 0, jnp.maximum(room, 0))
    moved = jax.random.randint(jax.random.fold_in(own, 4), (amount // 2,), 0, 1 << 20) % (room + 1)
    tallies = tallies.at[source_of].add(-moved).at[taker].add(moved)
    labels = jnp.searchsorted(jnp.cumsum(tallies), jnp.arange(rows * top), side="right").astype(jnp.int32)
    table = labels.reshape(top, rows).T
    table = table[jax.random.permutation(jax.random.fold_in(own, 1), rows)]
    offset_by = jax.random.randint(jax.random.fold_in(own, 2), (rows, 1), 0, top)
    return jnp.take_along_axis(table, (jnp.arange(top)[None, :] + offset_by) % top, axis=1)


def portions_of(amount, total, reach, skew, full):
    weights = [(1 << 20) // math.isqrt(rank ** skew) + 1 for rank in range(1, amount + 1)]
    largest = reach if full else min(reach, max(-(-total // amount), total * weights[0] // sum(weights)))
    least = 1 if total - largest >= amount - 1 else 0
    counts, spare = [largest] + [least] * (amount - 1), total - largest - least * (amount - 1)
    while spare > 0:
        movable = [i for i in range(1, amount) if counts[i] < largest] or [i for i in range(1, amount) if counts[i] < reach]
        pool, left = sum([weights[i] for i in movable]), spare
        for i in movable:
            addition = min(reach - counts[i], max(1, left * weights[i] // pool), spare)
            counts[i] = counts[i] + addition
            spare = spare - addition
    return np.array(counts)


def noise(rng, extent, spread, limit, cuts=(), held_as=jnp.bfloat16):
    loudness = block_scale(rng, extent, cuts, -0.22, 0.18) if cuts else 1.0
    array = jax.random.normal(rng, extent, jnp.float32) * spread * loudness
    return jnp.minimum(jnp.maximum(array, -limit), limit).astype(held_as)


def setup_inputs(seed: int = 0) -> dict:
    arg_keys = jax.random.split(jax.random.key(seed), 4)
    grad_parts = noise(arg_keys[0], (N_DP, NB, BLK, BLK), 1.0, 6.0, ((0, 4), (1, 8), (2, 32)))
    owner_ids_keys = jax.random.split(jax.random.fold_in(arg_keys[1], 1), NB // NBD)
    owner_ids_turns = jax.random.permutation(jax.random.fold_in(arg_keys[1], 3), NB // NBD)
    owner_ids = jax.vmap(lambda own, number: shared_out(jax.random.fold_in(arg_keys[1], 2), own, number, NBD, N_FSDP, 1, CAP, 2))(owner_ids_keys, owner_ids_turns).reshape((NB, 1))
    factors = draw_factors(jax.random.fold_in(arg_keys[3], 71), 0)
    return dict(grad_parts=grad_parts, owner_ids=owner_ids, factors=factors)


decay_rate = 0.95
epsilon = 1e-06

def slot_ranks(owners):
    positions = jnp.arange(owners.shape[0])
    same_owner = owners[:, None] == owners[None, :]
    earlier = positions[None, :] < positions[:, None]
    return lax.optimization_barrier(jnp.sum(jnp.where(same_owner & earlier, 1, 0), axis=1)).astype(jnp.int32)

def batched_product(first_term, second_term):
    return jnp.einsum('sij,sjk->sik', first_term, second_term, precision=lax.Precision.HIGHEST)

def inverse_root(factor):
    row_bound = lax.optimization_barrier(jnp.max(lax.optimization_barrier(jnp.sum(jnp.abs(factor), axis=2)), axis=1)) + epsilon
    normed = factor / row_bound[:, None, None]
    identity = jnp.eye(factor.shape[1], dtype=jnp.float32)
    first_step = (5.0 * identity - normed) * 0.25
    squared = batched_product(first_step, first_step)
    fourth_power = batched_product(squared, squared)
    shifted = batched_product(fourth_power, normed)
    second_step = (5.0 * identity - shifted) * 0.25
    return batched_product(first_step, second_step)

def precondition(blocks, left_prev, right_prev, used_slots):
    widened = blocks.astype(jnp.float32)
    left_factor = decay_rate * left_prev + jnp.einsum('sij,skj->sik', widened, widened, precision=lax.Precision.HIGHEST)
    right_factor = decay_rate * right_prev + jnp.einsum('sji,sjk->sik', widened, widened, precision=lax.Precision.HIGHEST)
    left_root = inverse_root(left_factor).astype(jnp.bfloat16)
    right_root = inverse_root(right_factor).astype(jnp.bfloat16)
    half_product = batched_product(left_root.astype(jnp.float32), widened).astype(jnp.bfloat16)
    raw_direction = batched_product(half_product.astype(jnp.float32), right_root.astype(jnp.float32))
    grad_scale = jnp.sqrt(lax.optimization_barrier(jnp.mean(widened * widened, axis=(1, 2))) + epsilon)
    own_scale = jnp.sqrt(lax.optimization_barrier(jnp.mean(raw_direction * raw_direction, axis=(1, 2))) + epsilon)
    direction = (raw_direction * (grad_scale / own_scale)[:, None, None]).astype(jnp.bfloat16)
    keep_mask = used_slots[:, None, None]
    return (jnp.where(keep_mask, left_factor, left_prev), jnp.where(keep_mask, right_factor, right_prev), direction)

def reference(grad_parts, owner_ids, factors):
    group_count = N_MP * N_DP
    group_grads = jnp.moveaxis(grad_parts.reshape(N_DP, group_count, NBD, BLK, BLK), 1, 0)
    owner_groups = owner_ids.reshape(group_count, NBD)
    slot_states = factors.reshape(group_count, N_FSDP * CAP, 2, BLK, BLK)

    def one_group(group_item):
        partials, owners, slot_state = group_item
        reduced = lax.optimization_barrier(jnp.sum(partials.astype(jnp.float32), axis=0)).astype(jnp.bfloat16)
        places = owners * CAP + slot_ranks(owners)
        buffer = jnp.zeros((N_FSDP * CAP, BLK, BLK), jnp.bfloat16).at[places].set(reduced)
        used_slots = jnp.zeros((N_FSDP * CAP,), jnp.int32).at[places].set(1) > 0
        left_new, right_new, direction = precondition(buffer, slot_state[:, 0], slot_state[:, 1], used_slots)
        return (jnp.stack([left_new, right_new], axis=1), direction[places])
    new_states, directions = lax.map(one_group, (group_grads, owner_groups, slot_states))
    return (directions.reshape(NB, BLK, BLK), new_states.reshape(factors.shape))
```

```python
import numpy as np
import jax
import jax.numpy as jnp
from jax import lax
from jax.experimental import pallas as pl
from jax.experimental.pallas import tpu as pltpu
from jax.sharding import PartitionSpec as P

decay_rate = 0.95
epsilon = 1e-06
centre = 0.5


def root_coefficients():
    x = np.polynomial.Polynomial([centre, 1.0])
    t0 = (5.0 - x) / 4.0
    t1 = (5.0 - t0**4 * x) / 4.0
    return [float(c) for c in (t0 * t1).coef]


def dot(a, b, contract):
    return lax.dot_general(a, b, ((contract[:1], contract[1:]), ((), ())), preferred_element_type=jnp.float32)


def inverse_root(factor, eye):
    r = root_coefficients()
    bound = jnp.max(jnp.sum(jnp.abs(factor), axis=0, keepdims=True), axis=1, keepdims=True) + epsilon
    m = factor * (1.0 / bound) - centre * eye
    mh = m.astype(jnp.bfloat16)
    m2 = dot(mh, mh, (1, 0))
    m2h = m2.astype(jnp.bfloat16)
    u = r[4] * eye + r[5] * m + r[6] * m2
    v = r[3] * m + dot(m2h, u.astype(jnp.bfloat16), (1, 0))
    return r[0] * eye + r[1] * m + r[2] * m2 + dot(m2h, v.astype(jnp.bfloat16), (1, 0))


def place_kernel(owners, parts, out, seen):
    out[...] = jnp.zeros_like(out)
    replicas, count = parts.shape[:2]
    first = lax.axis_index("dp") * count

    def clear(i, _):
        seen[i] = 0
        return 0

    lax.fori_loop(0, out.shape[0], clear, 0)

    def step(b, _):
        owner = owners[first + b]
        slot = seen[owner]
        seen[owner] = slot + 1
        total = parts[0, b].astype(jnp.float32)
        for r in range(1, replicas):
            total = total + parts[r, b].astype(jnp.float32)
        out[owner, slot] = total.astype(out.dtype)
        return 0

    lax.fori_loop(0, count, step, 0, unroll=True)


def pick_kernel(owners, rows, out, seen):
    count = out.shape[0]
    first = lax.axis_index("dp") * count

    def clear(i, _):
        seen[i] = 0
        return 0

    lax.fori_loop(0, rows.shape[0], clear, 0)

    def step(b, _):
        owner = owners[first + b]
        slot = seen[owner]
        seen[owner] = slot + 1
        out[b] = rows[owner, slot]
        return 0

    lax.fori_loop(0, count, step, 0, unroll=True)


def precondition_kernel(owners, rows, factors, out, state):
    count = rows.shape[0]
    first = lax.axis_index("dp") * count
    me = lax.axis_index("fsdp")
    order = factors.shape[-1]
    live = lax.fori_loop(0, count, lambda b, n: n + jnp.where(owners[first + b] == me, 1, 0), 0, unroll=True)
    eye = (
        lax.broadcasted_iota(jnp.int32, (order, order), 0) == lax.broadcasted_iota(jnp.int32, (order, order), 1)
    ).astype(jnp.float32)
    for s in range(factors.shape[0]):
        wide = rows[:, s].astype(jnp.float32).reshape(order, order)
        g = wide.astype(jnp.bfloat16)
        left = decay_rate * factors[s, 0] + dot(g, g, (1, 1))
        right = decay_rate * factors[s, 1] + dot(g, g, (0, 0))
        used = s < live
        state[s, 0] = jnp.where(used, left, factors[s, 0])
        state[s, 1] = jnp.where(used, right, factors[s, 1])
        left_root = inverse_root(left, eye).astype(jnp.bfloat16)
        right_root = inverse_root(right, eye).astype(jnp.bfloat16)
        half = dot(left_root, g, (1, 0)).astype(jnp.bfloat16)
        raw = dot(half, right_root, (1, 0))

        def mean_square(x):
            return jnp.sum(jnp.sum(x * x, axis=0, keepdims=True), axis=1, keepdims=True) / (order * order)

        ratio = jnp.sqrt(mean_square(wide) + epsilon) / jnp.sqrt(mean_square(raw) + epsilon)
        out[:, s] = (raw * ratio).reshape(rows.shape[0], rows.shape[2], order).astype(out.dtype)


def body(grad_parts, owner_ids, factors):
    fsdp_count = lax.axis_size("fsdp")
    replica_count = lax.axis_size("dp")
    slot_count = factors.shape[2]
    row_count, width = grad_parts.shape[2:]
    group_blocks = grad_parts.shape[1] // replica_count
    owners = owner_ids.reshape(-1)
    vmem = pl.BlockSpec(memory_space=pltpu.VMEM)
    smem = pl.BlockSpec(memory_space=pltpu.SMEM)
    seen = pltpu.SMEM((fsdp_count,), jnp.int32)
    params = pltpu.CompilerParams(vmem_limit_bytes=32 * 1024 * 1024)
    wire = jax.ShapeDtypeStruct((fsdp_count, slot_count, row_count, width), jnp.bfloat16)

    mine = grad_parts.reshape(replica_count, group_blocks, row_count, width)
    parts = lax.all_to_all(mine, "dp", split_axis=0, concat_axis=0, tiled=True)
    outgoing = pl.pallas_call(
        place_kernel,
        out_shape=wire,
        in_specs=[smem, vmem],
        out_specs=vmem,
        scratch_shapes=[seen],
        compiler_params=params,
        name="sum_and_place",
    )(owners, parts)
    arrived = lax.all_to_all(outgoing, "fsdp", split_axis=0, concat_axis=0, tiled=True)
    directions, state = pl.pallas_call(
        precondition_kernel,
        out_shape=(wire, jax.ShapeDtypeStruct(factors.shape[2:], factors.dtype)),
        in_specs=[smem, vmem, vmem],
        out_specs=(vmem, vmem),
        compiler_params=params,
        name="precondition",
    )(owners, arrived, factors[0, 0])
    returned = lax.all_to_all(directions, "fsdp", split_axis=0, concat_axis=0, tiled=True)
    picked = pl.pallas_call(
        pick_kernel,
        out_shape=jax.ShapeDtypeStruct((group_blocks, row_count, width), jnp.bfloat16),
        in_specs=[smem, vmem],
        out_specs=vmem,
        scratch_shapes=[seen],
        compiler_params=params,
        name="pick",
    )(owners, returned)
    gathered = lax.all_gather(picked, "dp", axis=0, tiled=True)
    return gathered, state[None, None]


def solution(mesh):
    return jax.shard_map(
        body,
        mesh=mesh,
        in_specs=(
            P("dp", "mp", "fsdp", None),
            P("mp", None),
            P("mp", "dp", "fsdp", None, None, None),
        ),
        out_specs=(P("mp", "fsdp", None), P("mp", "dp", "fsdp", None, None, None)),
        check_vma=False,
    )
```

```python
import numpy as np
import jax
import jax.numpy as jnp
from jax import lax
from jax.experimental import pallas as pl
from jax.experimental.pallas import tpu as pltpu
from jax.sharding import PartitionSpec as P

decay_rate = 0.95
epsilon = 1e-06
centre = 0.5


def root_coefficients():
    x = np.polynomial.Polynomial([centre, 1.0])
    t0 = (5.0 - x) / 4.0
    t1 = (5.0 - t0**4 * x) / 4.0
    return [float(c) for c in (t0 * t1).coef]


def dot(a, b, contract):
    return lax.dot_general(a, b, ((contract[:1], contract[1:]), ((), ())), preferred_element_type=jnp.float32)


def mean_square(x):
    return jnp.sum(jnp.sum(x * x, axis=0, keepdims=True), axis=1, keepdims=True) / x.size


def next_place(owners, seen, b):
    owner = owners[b]
    slot = seen[owner]
    seen[owner] = slot + 1
    return owner, slot


def place_kernel(owners_hbm, parts, out, owners, seen, total, sem):
    fetch = pltpu.make_async_copy(owners_hbm, owners, sem)
    fetch.start()
    replicas, count = parts.shape[:2]
    for b in range(count):
        row_sum = parts[0, b].astype(jnp.float32)
        for r in range(1, replicas):
            row_sum = row_sum + parts[r, b].astype(jnp.float32)
        total[b] = row_sum.astype(total.dtype)
    out[...] = jnp.zeros_like(out)
    for i in range(out.shape[0]):
        seen[i] = 0
    first = lax.axis_index("dp") * count
    fetch.wait()
    for b in range(count):
        owner, slot = next_place(owners, seen, first + b)
        out[owner, slot] = total[b]


def pick_kernel(owners, rows, out, seen):
    replicas, count = out.shape[:2]
    for i in range(rows.shape[0]):
        seen[i] = 0
    first = lax.axis_index("dp") * count
    for b in range(count):
        owner, slot = next_place(owners, seen, first + b)
        block = rows[owner, slot]
        for r in range(replicas):
            out[r, b] = block


def precondition_kernel(owners, rows, factors, out, state):
    count, slots = rows.shape[:2]
    order = factors.shape[-1]
    first = lax.axis_index("dp") * count
    me = lax.axis_index("fsdp")
    live = jnp.int32(0)
    for b in range(count):
        live = live + jnp.where(owners[first + b] == me, 1, 0)
    r = root_coefficients()
    half_type = jnp.bfloat16
    diagonal = lax.broadcasted_iota(jnp.int32, (order, order), 0) == lax.broadcasted_iota(
        jnp.int32, (order, order), 1
    )
    wide = [rows[:, s].astype(jnp.float32).reshape(order, order) for s in range(slots)]
    g = [w.astype(half_type) for w in wide]
    pairs = [(s, side) for s in range(slots) for side in range(2)]
    factor = []
    for s, side in pairs:
        gram = dot(g[s], g[s], (1, 1) if side == 0 else (0, 0))
        factor.append(decay_rate * factors[s, side] + gram)
        state[s, side] = jnp.where(s < live, factor[-1], factors[s, side])
    bound = [jnp.max(jnp.sum(jnp.abs(a), axis=0, keepdims=True), axis=1, keepdims=True) + epsilon for a in factor]
    m = [a * (1.0 / c) - jnp.where(diagonal, centre, 0.0) for a, c in zip(factor, bound)]
    mh = [x.astype(half_type) for x in m]
    m2 = [dot(x, x, (1, 0)) for x in mh]
    m2h = [x.astype(half_type) for x in m2]
    u = [(r[5] * x + r[6] * y).astype(half_type) for x, y in zip(m, m2)]
    w = [dot(x, y, (1, 0)) for x, y in zip(m2h, u)]
    v = [(r[3] * x + r[4] * y + z).astype(half_type) for x, y, z in zip(m, m2, w)]
    p = [dot(x, y, (1, 0)) for x, y in zip(m2h, v)]
    root = [
        (jnp.where(diagonal, r[0], 0.0) + r[1] * x + r[2] * y + z).astype(half_type) for x, y, z in zip(m, m2, p)
    ]
    for s in range(slots):
        half = dot(root[2 * s], g[s], (1, 0)).astype(half_type)
        raw = dot(half, root[2 * s + 1], (1, 0))
        ratio = jnp.sqrt(mean_square(wide[s]) + epsilon) / jnp.sqrt(mean_square(raw) + epsilon)
        out[:, s] = (raw * ratio).reshape(count, rows.shape[2], order).astype(out.dtype)


def body(grad_parts, owner_ids, factors):
    fsdp_count = lax.axis_size("fsdp")
    replica_count = lax.axis_size("dp")
    slot_count = factors.shape[2]
    row_count, width = grad_parts.shape[2:]
    group_blocks = grad_parts.shape[1] // replica_count
    owners = owner_ids.reshape(-1)
    vmem = pl.BlockSpec(memory_space=pltpu.VMEM)
    smem = pl.BlockSpec(memory_space=pltpu.SMEM)
    seen = pltpu.SMEM((fsdp_count,), jnp.int32)
    params = pltpu.CompilerParams(vmem_limit_bytes=32 * 1024 * 1024)
    wire = jax.ShapeDtypeStruct((fsdp_count, slot_count, row_count, width), jnp.bfloat16)

    mine = grad_parts.reshape(replica_count, group_blocks, row_count, width)
    parts = lax.all_to_all(mine, "dp", split_axis=0, concat_axis=0, tiled=True)
    outgoing = pl.pallas_call(
        place_kernel,
        out_shape=wire,
        in_specs=[pl.BlockSpec(memory_space=pltpu.HBM), vmem],
        out_specs=vmem,
        scratch_shapes=[
            pltpu.SMEM(owners.shape, jnp.int32),
            seen,
            pltpu.VMEM(mine.shape[1:], jnp.bfloat16),
            pltpu.SemaphoreType.DMA,
        ],
        compiler_params=params,
        name="sum_and_place",
    )(pltpu.with_memory_space_constraint(owners, pltpu.HBM), parts)
    arrived = lax.all_to_all(outgoing, "fsdp", split_axis=0, concat_axis=0, tiled=True)
    directions, state = pl.pallas_call(
        precondition_kernel,
        out_shape=(wire, jax.ShapeDtypeStruct(factors.shape[2:], factors.dtype)),
        in_specs=[smem, vmem, vmem],
        out_specs=(vmem, vmem),
        compiler_params=params,
        name="precondition",
    )(owners, arrived, factors[0, 0])
    returned = lax.all_to_all(directions, "fsdp", split_axis=0, concat_axis=0, tiled=True)
    picked = pl.pallas_call(
        pick_kernel,
        out_shape=jax.ShapeDtypeStruct(mine.shape, jnp.bfloat16),
        in_specs=[smem, vmem],
        out_specs=vmem,
        scratch_shapes=[seen],
        compiler_params=params,
        name="pick",
    )(owners, returned)
    gathered = lax.all_to_all(picked, "dp", split_axis=0, concat_axis=0, tiled=True)
    return gathered.reshape(grad_parts.shape[1:]), state[None, None]


def solution(mesh):
    return jax.shard_map(
        body,
        mesh=mesh,
        in_specs=(
            P("dp", "mp", "fsdp", None),
            P("mp", None),
            P("mp", "dp", "fsdp", None, None, None),
        ),
        out_specs=(P("mp", "fsdp", None), P("mp", "dp", "fsdp", None, None, None)),
        check_vma=False,
    )
```

```python
import numpy as np
import jax
import jax.numpy as jnp
from jax import lax
from jax.experimental import pallas as pl
from jax.experimental.pallas import tpu as pltpu
from jax.sharding import PartitionSpec as P

decay_rate = 0.95
epsilon = 1e-06
centre = 0.5


def root_coefficients():
    x = np.polynomial.Polynomial([centre, 1.0])
    t0 = (5.0 - x) / 4.0
    t1 = (5.0 - t0**4 * x) / 4.0
    return [float(c) for c in (t0 * t1).coef]


def dot(a, b, contract):
    return lax.dot_general(a, b, ((contract[:1], contract[1:]), ((), ())), preferred_element_type=jnp.float32)


def mean_square(x):
    return jnp.sum(jnp.sum(x * x, axis=0, keepdims=True), axis=1, keepdims=True) / x.size


def place_kernel(owners_hbm, parts, out, places, owners, seen, total, sem):
    fetch = pltpu.make_async_copy(owners_hbm, owners, sem)
    fetch.start()
    replicas, count = parts.shape[:2]
    for b in range(count):
        row_sum = parts[0, b].astype(jnp.float32)
        for r in range(1, replicas):
            row_sum = row_sum + parts[r, b].astype(jnp.float32)
        total[b] = row_sum.astype(total.dtype)
    out[...] = jnp.zeros_like(out)
    for i in range(out.shape[0]):
        seen[i] = 0
    first = lax.axis_index("dp") * count
    fetch.wait()
    for b in range(count):
        owner = owners[first + b]
        slot = seen[owner]
        seen[owner] = slot + 1
        places[b] = owner * out.shape[1] + slot
        out[owner, slot] = total[b]


def pick_kernel(places, rows, out):
    replicas, count = out.shape[:2]
    slots = rows.shape[1]
    for b in range(count):
        block = rows[places[b] // slots, places[b] % slots]
        for r in range(replicas):
            out[r, b] = block


def precondition_kernel(places, rows, factors, out, state):
    count, slots = rows.shape[:2]
    order = factors.shape[-1]
    me = lax.axis_index("fsdp")
    live = jnp.int32(0)
    for b in range(count):
        live = live + jnp.where(places[b] // slots == me, 1, 0)
    r = root_coefficients()
    half_type = jnp.bfloat16
    diagonal = lax.broadcasted_iota(jnp.int32, (order, order), 0) == lax.broadcasted_iota(
        jnp.int32, (order, order), 1
    )
    wide = [rows[:, s].astype(jnp.float32).reshape(order, order) for s in range(slots)]
    g = [w.astype(half_type) for w in wide]
    pairs = [(s, side) for s in range(slots) for side in range(2)]
    factor = []
    for s, side in pairs:
        gram = dot(g[s], g[s], (1, 1) if side == 0 else (0, 0))
        factor.append(decay_rate * factors[s, side] + gram)
        state[s, side] = jnp.where(s < live, factor[-1], factors[s, side])
    bound = [jnp.max(jnp.sum(jnp.abs(a), axis=0, keepdims=True), axis=1, keepdims=True) + epsilon for a in factor]
    m = [a * (1.0 / c) - jnp.where(diagonal, centre, 0.0) for a, c in zip(factor, bound)]
    mh = [x.astype(half_type) for x in m]
    m2 = [dot(x, x, (1, 0)) for x in mh]
    m2h = [x.astype(half_type) for x in m2]
    u = [(r[5] * x + r[6] * y).astype(half_type) for x, y in zip(m, m2)]
    w = [dot(x, y, (1, 0)) for x, y in zip(m2h, u)]
    v = [(r[3] * x + r[4] * y + z).astype(half_type) for x, y, z in zip(m, m2, w)]
    p = [dot(x, y, (1, 0)) for x, y in zip(m2h, v)]
    root = [
        (jnp.where(diagonal, r[0], 0.0) + r[1] * x + r[2] * y + z).astype(half_type) for x, y, z in zip(m, m2, p)
    ]
    for s in range(slots):
        half = dot(root[2 * s], g[s], (1, 0)).astype(half_type)
        raw = dot(half, root[2 * s + 1], (1, 0))
        ratio = jnp.sqrt(mean_square(wide[s]) + epsilon) / jnp.sqrt(mean_square(raw) + epsilon)
        out[:, s] = (raw * ratio).reshape(count, rows.shape[2], order).astype(out.dtype)


def body(grad_parts, owner_ids, factors):
    fsdp_count = lax.axis_size("fsdp")
    replica_count = lax.axis_size("dp")
    slot_count = factors.shape[2]
    row_count, width = grad_parts.shape[2:]
    group_blocks = grad_parts.shape[1] // replica_count
    owners = owner_ids.reshape(-1)
    vmem = pl.BlockSpec(memory_space=pltpu.VMEM)
    smem = pl.BlockSpec(memory_space=pltpu.SMEM)
    params = pltpu.CompilerParams(vmem_limit_bytes=32 * 1024 * 1024)
    wire = jax.ShapeDtypeStruct((fsdp_count, slot_count, row_count, width), jnp.bfloat16)

    mine = grad_parts.reshape(replica_count, group_blocks, row_count, width)
    parts = lax.all_to_all(mine, "dp", split_axis=0, concat_axis=0, tiled=True)
    outgoing, places = pl.pallas_call(
        place_kernel,
        out_shape=(wire, jax.ShapeDtypeStruct((group_blocks,), jnp.int32)),
        in_specs=[pl.BlockSpec(memory_space=pltpu.HBM), vmem],
        out_specs=(vmem, smem),
        scratch_shapes=[
            pltpu.SMEM(owners.shape, jnp.int32),
            pltpu.SMEM((fsdp_count,), jnp.int32),
            pltpu.VMEM(mine.shape[1:], jnp.bfloat16),
            pltpu.SemaphoreType.DMA,
        ],
        compiler_params=params,
        name="sum_and_place",
    )(pltpu.with_memory_space_constraint(owners, pltpu.HBM), parts)
    arrived = lax.all_to_all(outgoing, "fsdp", split_axis=0, concat_axis=0, tiled=True)
    directions, state = pl.pallas_call(
        precondition_kernel,
        out_shape=(wire, jax.ShapeDtypeStruct(factors.shape[2:], factors.dtype)),
        in_specs=[smem, vmem, vmem],
        out_specs=(vmem, vmem),
        compiler_params=params,
        name="precondition",
    )(places, arrived, factors[0, 0])
    returned = lax.all_to_all(directions, "fsdp", split_axis=0, concat_axis=0, tiled=True)
    picked = pl.pallas_call(
        pick_kernel,
        out_shape=jax.ShapeDtypeStruct(mine.shape, jnp.bfloat16),
        in_specs=[smem, vmem],
        out_specs=vmem,
        compiler_params=params,
        name="pick",
    )(places, returned)
    gathered = lax.all_to_all(picked, "dp", split_axis=0, concat_axis=0, tiled=True)
    return gathered.reshape(grad_parts.shape[1:]), state[None, None]


def solution(mesh):
    return jax.shard_map(
        body,
        mesh=mesh,
        in_specs=(
            P("dp", "mp", "fsdp", None),
            P("mp", None),
            P("mp", "dp", "fsdp", None, None, None),
        ),
        out_specs=(P("mp", "fsdp", None), P("mp", "dp", "fsdp", None, None, None)),
        check_vma=False,
    )
```

```python
import numpy as np
import jax
import jax.numpy as jnp
from jax import lax
from jax.experimental import pallas as pl
from jax.experimental.pallas import tpu as pltpu
from jax.sharding import PartitionSpec as P

decay_rate = 0.95
epsilon = 1e-06
centre = 0.5


def root_coefficients():
    x = np.polynomial.Polynomial([centre, 1.0])
    t0 = (5.0 - x) / 4.0
    t1 = (5.0 - t0**4 * x) / 4.0
    return [float(c) for c in (t0 * t1).coef]


def dot(a, b, contract):
    return lax.dot_general(a, b, ((contract[:1], contract[1:]), ((), ())), preferred_element_type=jnp.float32)


def mean_square(x):
    return jnp.sum(jnp.sum(x * x, axis=0, keepdims=True), axis=1, keepdims=True) / x.size


def next_place(owners, seen, b):
    owner = owners[b]
    slot = seen[owner]
    seen[owner] = slot + 1
    return owner, slot


def place_kernel(owners_hbm, parts, out, kept_owners, owners, seen, total, sem):
    fetch = pltpu.make_async_copy(owners_hbm, owners, sem.at[0])
    fetch.start()
    keep = pltpu.make_async_copy(owners_hbm, kept_owners, sem.at[1])
    keep.start()
    replicas, count = parts.shape[:2]
    for b in range(count):
        row_sum = parts[0, b].astype(jnp.float32)
        for r in range(1, replicas):
            row_sum = row_sum + parts[r, b].astype(jnp.float32)
        total[b] = row_sum.astype(total.dtype)
    out[...] = jnp.zeros_like(out)
    for i in range(out.shape[0]):
        seen[i] = 0
    first = lax.axis_index("dp") * count
    fetch.wait()
    for b in range(count):
        owner, slot = next_place(owners, seen, first + b)
        out[owner, slot] = total[b]
    keep.wait()


def pick_kernel(owners, rows, out, seen):
    replicas, count = out.shape[:2]
    for i in range(rows.shape[0]):
        seen[i] = 0
    first = lax.axis_index("dp") * count
    for b in range(count):
        owner, slot = next_place(owners, seen, first + b)
        block = rows[owner, slot]
        for r in range(replicas):
            out[r, b] = block


def precondition_kernel(owners, rows, factors, out, state):
    count, slots = rows.shape[:2]
    order = factors.shape[-1]
    first = lax.axis_index("dp") * count
    me = lax.axis_index("fsdp")
    live = jnp.int32(0)
    for b in range(count):
        live = live + jnp.where(owners[first + b] == me, 1, 0)
    r = root_coefficients()
    half_type = jnp.bfloat16
    diagonal = lax.broadcasted_iota(jnp.int32, (order, order), 0) == lax.broadcasted_iota(
        jnp.int32, (order, order), 1
    )
    wide = [rows[:, s].astype(jnp.float32).reshape(order, order) for s in range(slots)]
    g = [w.astype(half_type) for w in wide]
    pairs = [(s, side) for s in range(slots) for side in range(2)]
    factor = []
    for s, side in pairs:
        gram = dot(g[s], g[s], (1, 1) if side == 0 else (0, 0))
        factor.append(decay_rate * factors[s, side] + gram)
        state[s, side] = jnp.where(s < live, factor[-1], factors[s, side])
    bound = [jnp.max(jnp.sum(jnp.abs(a), axis=0, keepdims=True), axis=1, keepdims=True) + epsilon for a in factor]
    m = [a * (1.0 / c) - jnp.where(diagonal, centre, 0.0) for a, c in zip(factor, bound)]
    mh = [x.astype(half_type) for x in m]
    m2 = [dot(x, x, (1, 0)) for x in mh]
    m2h = [x.astype(half_type) for x in m2]
    u = [(r[5] * x + r[6] * y).astype(half_type) for x, y in zip(m, m2)]
    w = [dot(x, y, (1, 0)) for x, y in zip(m2h, u)]
    v = [(r[3] * x + r[4] * y + z).astype(half_type) for x, y, z in zip(m, m2, w)]
    p = [dot(x, y, (1, 0)) for x, y in zip(m2h, v)]
    root = [
        (jnp.where(diagonal, r[0], 0.0) + r[1] * x + r[2] * y + z).astype(half_type) for x, y, z in zip(m, m2, p)
    ]
    for s in range(slots):
        half = dot(root[2 * s], g[s], (1, 0)).astype(half_type)
        raw = dot(half, root[2 * s + 1], (1, 0))
        ratio = jnp.sqrt(mean_square(wide[s]) + epsilon) / jnp.sqrt(mean_square(raw) + epsilon)
        out[:, s] = (raw * ratio).reshape(count, rows.shape[2], order).astype(out.dtype)


def body(grad_parts, owner_ids, factors):
    fsdp_count = lax.axis_size("fsdp")
    replica_count = lax.axis_size("dp")
    slot_count = factors.shape[2]
    row_count, width = grad_parts.shape[2:]
    group_blocks = grad_parts.shape[1] // replica_count
    owners = owner_ids.reshape(-1)
    vmem = pl.BlockSpec(memory_space=pltpu.VMEM)
    smem = pl.BlockSpec(memory_space=pltpu.SMEM)
    seen = pltpu.SMEM((fsdp_count,), jnp.int32)
    params = pltpu.CompilerParams(vmem_limit_bytes=32 * 1024 * 1024)
    wire = jax.ShapeDtypeStruct((fsdp_count, slot_count, row_count, width), jnp.bfloat16)

    mine = grad_parts.reshape(replica_count, group_blocks, row_count, width)
    parts = lax.all_to_all(mine, "dp", split_axis=0, concat_axis=0, tiled=True)
    outgoing, kept_owners = pl.pallas_call(
        place_kernel,
        out_shape=(wire, pltpu.VMEM(owners.shape, jnp.int32)),
        in_specs=[pl.BlockSpec(memory_space=pltpu.HBM), vmem],
        out_specs=(vmem, vmem),
        scratch_shapes=[
            pltpu.SMEM(owners.shape, jnp.int32),
            seen,
            pltpu.VMEM(mine.shape[1:], jnp.bfloat16),
            pltpu.SemaphoreType.DMA((2,)),
        ],
        compiler_params=params,
        name="sum_and_place",
    )(pltpu.with_memory_space_constraint(owners, pltpu.HBM), parts)
    arrived = lax.all_to_all(outgoing, "fsdp", split_axis=0, concat_axis=0, tiled=True)
    directions, state = pl.pallas_call(
        precondition_kernel,
        out_shape=(wire, jax.ShapeDtypeStruct(factors.shape[2:], factors.dtype)),
        in_specs=[smem, vmem, vmem],
        out_specs=(vmem, vmem),
        compiler_params=params,
        name="precondition",
    )(kept_owners, arrived, factors[0, 0])
    returned = lax.all_to_all(directions, "fsdp", split_axis=0, concat_axis=0, tiled=True)
    picked = pl.pallas_call(
        pick_kernel,
        out_shape=jax.ShapeDtypeStruct(mine.shape, jnp.bfloat16),
        in_specs=[smem, vmem],
        out_specs=vmem,
        scratch_shapes=[seen],
        compiler_params=params,
        name="pick",
    )(kept_owners, returned)
    gathered = lax.all_to_all(picked, "dp", split_axis=0, concat_axis=0, tiled=True)
    return gathered.reshape(grad_parts.shape[1:]), state[None, None]


def solution(mesh):
    return jax.shard_map(
        body,
        mesh=mesh,
        in_specs=(
            P("dp", "mp", "fsdp", None),
            P("mp", None),
            P("mp", "dp", "fsdp", None, None, None),
        ),
        out_specs=(P("mp", "fsdp", None), P("mp", "dp", "fsdp", None, None, None)),
        check_vma=False,
    )
```

```python
import numpy as np
import jax
import jax.numpy as jnp
from jax import lax
from jax.experimental import pallas as pl
from jax.experimental.pallas import tpu as pltpu
from jax.sharding import PartitionSpec as P

decay_rate = 0.95
epsilon = 1e-06
centre = 0.5


def root_coefficients():
    x = np.polynomial.Polynomial([centre, 1.0])
    t0 = (5.0 - x) / 4.0
    t1 = (5.0 - t0**4 * x) / 4.0
    return [float(c) for c in (t0 * t1).coef]


def dot(a, b, contract):
    return lax.dot_general(a, b, ((contract[:1], contract[1:]), ((), ())), preferred_element_type=jnp.float32)


def mean_square(x):
    return jnp.sum(jnp.sum(x * x, axis=0, keepdims=True), axis=1, keepdims=True) / x.size


def next_place(owners, seen, b):
    owner = owners[b]
    slot = seen[owner]
    seen[owner] = slot + 1
    return owner, slot


def place_kernel(owners_hbm, parts, out, kept_owners, used, owners, seen, total, sem):
    fetch = pltpu.make_async_copy(owners_hbm, owners, sem.at[0])
    fetch.start()
    keep = pltpu.make_async_copy(owners_hbm, kept_owners, sem.at[1])
    keep.start()
    replicas, count = parts.shape[:2]
    for b in range(count):
        row_sum = parts[0, b].astype(jnp.float32)
        for r in range(1, replicas):
            row_sum = row_sum + parts[r, b].astype(jnp.float32)
        total[b] = row_sum.astype(total.dtype)
    out[...] = jnp.zeros_like(out)
    for i in range(out.shape[0]):
        seen[i] = 0
    first = lax.axis_index("dp") * count
    fetch.wait()
    for b in range(count):
        owner, slot = next_place(owners, seen, first + b)
        out[owner, slot] = total[b]
    live = seen[lax.axis_index("fsdp")]
    for s in range(used.shape[0]):
        used[s : s + 1, :] = jnp.full((1, used.shape[1]), jnp.where(s < live, 1.0, 0.0), used.dtype)
    keep.wait()


def pick_kernel(owners, rows, out, seen):
    replicas, count = out.shape[:2]
    for i in range(rows.shape[0]):
        seen[i] = 0
    first = lax.axis_index("dp") * count
    for b in range(count):
        owner, slot = next_place(owners, seen, first + b)
        block = rows[owner, slot]
        for r in range(replicas):
            out[r, b] = block


def precondition_kernel(used, rows, factors, out, state):
    count, slots = rows.shape[:2]
    order = factors.shape[-1]
    r = root_coefficients()
    half_type = jnp.bfloat16
    diagonal = lax.broadcasted_iota(jnp.int32, (order, order), 0) == lax.broadcasted_iota(
        jnp.int32, (order, order), 1
    )
    wide = [rows[:, s].astype(jnp.float32).reshape(order, order) for s in range(slots)]
    g = [w.astype(half_type) for w in wide]
    pairs = [(s, side) for s in range(slots) for side in range(2)]
    factor = []
    for s, side in pairs:
        gram = dot(g[s], g[s], (1, 1) if side == 0 else (0, 0))
        factor.append(decay_rate * factors[s, side] + gram)
        state[s, side] = jnp.where(used[s : s + 1, :] > 0.0, factor[-1], factors[s, side])
    bound = [jnp.max(jnp.sum(jnp.abs(a), axis=0, keepdims=True), axis=1, keepdims=True) + epsilon for a in factor]
    m = [a * (1.0 / c) - jnp.where(diagonal, centre, 0.0) for a, c in zip(factor, bound)]
    mh = [x.astype(half_type) for x in m]
    m2 = [dot(x, x, (1, 0)) for x in mh]
    m2h = [x.astype(half_type) for x in m2]
    u = [(r[5] * x + r[6] * y).astype(half_type) for x, y in zip(m, m2)]
    w = [dot(x, y, (1, 0)) for x, y in zip(m2h, u)]
    v = [(r[3] * x + r[4] * y + z).astype(half_type) for x, y, z in zip(m, m2, w)]
    p = [dot(x, y, (1, 0)) for x, y in zip(m2h, v)]
    root = [
        (jnp.where(diagonal, r[0], 0.0) + r[1] * x + r[2] * y + z).astype(half_type) for x, y, z in zip(m, m2, p)
    ]
    for s in range(slots):
        half = dot(root[2 * s], g[s], (1, 0)).astype(half_type)
        raw = dot(half, root[2 * s + 1], (1, 0))
        ratio = jnp.sqrt(mean_square(wide[s]) + epsilon) / jnp.sqrt(mean_square(raw) + epsilon)
        out[:, s] = (raw * ratio).reshape(count, rows.shape[2], order).astype(out.dtype)


def body(grad_parts, owner_ids, factors):
    fsdp_count = lax.axis_size("fsdp")
    replica_count = lax.axis_size("dp")
    slot_count = factors.shape[2]
    row_count, width = grad_parts.shape[2:]
    group_blocks = grad_parts.shape[1] // replica_count
    owners = owner_ids.reshape(-1)
    vmem = pl.BlockSpec(memory_space=pltpu.VMEM)
    smem = pl.BlockSpec(memory_space=pltpu.SMEM)
    seen = pltpu.SMEM((fsdp_count,), jnp.int32)
    params = pltpu.CompilerParams(vmem_limit_bytes=32 * 1024 * 1024)
    wire = jax.ShapeDtypeStruct((fsdp_count, slot_count, row_count, width), jnp.bfloat16)

    mine = grad_parts.reshape(replica_count, group_blocks, row_count, width)
    parts = lax.all_to_all(mine, "dp", split_axis=0, concat_axis=0, tiled=True)
    outgoing, kept_owners, used = pl.pallas_call(
        place_kernel,
        out_shape=(
            wire,
            pltpu.VMEM(owners.shape, jnp.int32),
            pltpu.VMEM((slot_count, factors.shape[-1]), jnp.float32),
        ),
        in_specs=[pl.BlockSpec(memory_space=pltpu.HBM), vmem],
        out_specs=(vmem, vmem, vmem),
        scratch_shapes=[
            pltpu.SMEM(owners.shape, jnp.int32),
            seen,
            pltpu.VMEM(mine.shape[1:], jnp.bfloat16),
            pltpu.SemaphoreType.DMA((2,)),
        ],
        compiler_params=params,
        name="sum_and_place",
    )(pltpu.with_memory_space_constraint(owners, pltpu.HBM), parts)
    arrived = lax.all_to_all(outgoing, "fsdp", split_axis=0, concat_axis=0, tiled=True)
    directions, state = pl.pallas_call(
        precondition_kernel,
        out_shape=(wire, jax.ShapeDtypeStruct(factors.shape[2:], factors.dtype)),
        in_specs=[vmem, vmem, vmem],
        out_specs=(vmem, vmem),
        compiler_params=params,
        name="precondition",
    )(used, arrived, factors[0, 0])
    returned = lax.all_to_all(directions, "fsdp", split_axis=0, concat_axis=0, tiled=True)
    picked = pl.pallas_call(
        pick_kernel,
        out_shape=jax.ShapeDtypeStruct(mine.shape, jnp.bfloat16),
        in_specs=[smem, vmem],
        out_specs=vmem,
        scratch_shapes=[seen],
        compiler_params=params,
        name="pick",
    )(kept_owners, returned)
    gathered = lax.all_to_all(picked, "dp", split_axis=0, concat_axis=0, tiled=True)
    return gathered.reshape(grad_parts.shape[1:]), state[None, None]


def solution(mesh):
    return jax.shard_map(
        body,
        mesh=mesh,
        in_specs=(
            P("dp", "mp", "fsdp", None),
            P("mp", None),
            P("mp", "dp", "fsdp", None, None, None),
        ),
        out_specs=(P("mp", "fsdp", None), P("mp", "dp", "fsdp", None, None, None)),
        check_vma=False,
    )
```

```python
import numpy as np
import jax
import jax.numpy as jnp
from jax import lax
from jax.experimental import pallas as pl
from jax.experimental.pallas import tpu as pltpu
from jax.sharding import PartitionSpec as P

decay_rate = 0.95
epsilon = 1e-06
centre = 0.5


def root_coefficients():
    x = np.polynomial.Polynomial([centre, 1.0])
    t0 = (5.0 - x) / 4.0
    t1 = (5.0 - t0**4 * x) / 4.0
    return [float(c) for c in (t0 * t1).coef]


def dot(a, b, contract):
    return lax.dot_general(a, b, ((contract[:1], contract[1:]), ((), ())), preferred_element_type=jnp.float32)


def mean_square(x):
    return jnp.sum(jnp.sum(x * x, axis=0, keepdims=True), axis=1, keepdims=True) / x.size


def next_place(owners, seen, b):
    owner = owners[b]
    slot = seen[owner]
    seen[owner] = slot + 1
    return owner, slot


def place_kernel(owners_hbm, parts, out, owners, used, seen, total, sem):
    fetch = pltpu.make_async_copy(owners_hbm, owners, sem)
    fetch.start()
    replicas, count = parts.shape[:2]
    for b in range(count):
        row_sum = parts[0, b].astype(jnp.float32)
        for r in range(1, replicas):
            row_sum = row_sum + parts[r, b].astype(jnp.float32)
        total[b] = row_sum.astype(total.dtype)
    out[...] = jnp.zeros_like(out)
    for i in range(out.shape[0]):
        seen[i] = 0
    first = lax.axis_index("dp") * count
    fetch.wait()
    for b in range(count):
        owner, slot = next_place(owners, seen, first + b)
        out[owner, slot] = total[b]
    live = seen[lax.axis_index("fsdp")]
    for s in range(used.shape[0]):
        used[s : s + 1, :] = jnp.full((1, used.shape[1]), jnp.where(s < live, 1.0, 0.0), used.dtype)


def pick_kernel(owners, rows, out, seen):
    replicas, count = out.shape[:2]
    for i in range(rows.shape[0]):
        seen[i] = 0
    first = lax.axis_index("dp") * count
    for b in range(count):
        owner, slot = next_place(owners, seen, first + b)
        block = rows[owner, slot]
        for r in range(replicas):
            out[r, b] = block


def precondition_kernel(used, rows, factors, out, state):
    count, slots = rows.shape[:2]
    order = factors.shape[-1]
    r = root_coefficients()
    half_type = jnp.bfloat16
    diagonal = lax.broadcasted_iota(jnp.int32, (order, order), 0) == lax.broadcasted_iota(
        jnp.int32, (order, order), 1
    )
    wide = [rows[:, s].astype(jnp.float32).reshape(order, order) for s in range(slots)]
    g = [w.astype(half_type) for w in wide]
    pairs = [(s, side) for s in range(slots) for side in range(2)]
    factor = []
    for s, side in pairs:
        gram = dot(g[s], g[s], (1, 1) if side == 0 else (0, 0))
        factor.append(decay_rate * factors[s, side] + gram)
        state[s, side] = jnp.where(used[s : s + 1, :] > 0.0, factor[-1], factors[s, side])
    bound = [jnp.max(jnp.sum(jnp.abs(a), axis=0, keepdims=True), axis=1, keepdims=True) + epsilon for a in factor]
    m = [a * (1.0 / c) - jnp.where(diagonal, centre, 0.0) for a, c in zip(factor, bound)]
    mh = [x.astype(half_type) for x in m]
    m2 = [dot(x, x, (1, 0)) for x in mh]
    m2h = [x.astype(half_type) for x in m2]
    u = [(r[5] * x + r[6] * y).astype(half_type) for x, y in zip(m, m2)]
    w = [dot(x, y, (1, 0)) for x, y in zip(m2h, u)]
    v = [(r[3] * x + r[4] * y + z).astype(half_type) for x, y, z in zip(m, m2, w)]
    p = [dot(x, y, (1, 0)) for x, y in zip(m2h, v)]
    root = [
        (jnp.where(diagonal, r[0], 0.0) + r[1] * x + r[2] * y + z).astype(half_type) for x, y, z in zip(m, m2, p)
    ]
    for s in range(slots):
        half = dot(root[2 * s], g[s], (1, 0)).astype(half_type)
        raw = dot(half, root[2 * s + 1], (1, 0))
        ratio = jnp.sqrt(mean_square(wide[s]) + epsilon) / jnp.sqrt(mean_square(raw) + epsilon)
        out[:, s] = (raw * ratio).reshape(count, rows.shape[2], order).astype(out.dtype)


def body(grad_parts, owner_ids, factors):
    fsdp_count = lax.axis_size("fsdp")
    replica_count = lax.axis_size("dp")
    slot_count = factors.shape[2]
    row_count, width = grad_parts.shape[2:]
    group_blocks = grad_parts.shape[1] // replica_count
    owners = owner_ids.reshape(-1)
    vmem = pl.BlockSpec(memory_space=pltpu.VMEM)
    smem = pl.BlockSpec(memory_space=pltpu.SMEM)
    seen = pltpu.SMEM((fsdp_count,), jnp.int32)
    params = pltpu.CompilerParams(vmem_limit_bytes=32 * 1024 * 1024)
    wire = jax.ShapeDtypeStruct((fsdp_count, slot_count, row_count, width), jnp.bfloat16)

    mine = grad_parts.reshape(replica_count, group_blocks, row_count, width)
    parts = lax.all_to_all(mine, "dp", split_axis=0, concat_axis=0, tiled=True)
    outgoing, known_owners, used = pl.pallas_call(
        place_kernel,
        out_shape=(
            wire,
            pltpu.SMEM(owners.shape, jnp.int32),
            pltpu.VMEM((slot_count, factors.shape[-1]), jnp.float32),
        ),
        in_specs=[pl.BlockSpec(memory_space=pltpu.HBM), vmem],
        out_specs=(vmem, smem, vmem),
        scratch_shapes=[
            seen,
            pltpu.VMEM(mine.shape[1:], jnp.bfloat16),
            pltpu.SemaphoreType.DMA,
        ],
        compiler_params=params,
        name="sum_and_place",
    )(pltpu.with_memory_space_constraint(owners, pltpu.HBM), parts)
    arrived = lax.all_to_all(outgoing, "fsdp", split_axis=0, concat_axis=0, tiled=True)
    directions, state = pl.pallas_call(
        precondition_kernel,
        out_shape=(wire, jax.ShapeDtypeStruct(factors.shape[2:], factors.dtype)),
        in_specs=[vmem, vmem, vmem],
        out_specs=(vmem, vmem),
        compiler_params=params,
        name="precondition",
    )(used, arrived, factors[0, 0])
    returned = lax.all_to_all(directions, "fsdp", split_axis=0, concat_axis=0, tiled=True)
    picked = pl.pallas_call(
        pick_kernel,
        out_shape=jax.ShapeDtypeStruct(mine.shape, jnp.bfloat16),
        in_specs=[smem, vmem],
        out_specs=vmem,
        scratch_shapes=[seen],
        compiler_params=params,
        name="pick",
    )(known_owners, returned)
    gathered = lax.all_to_all(picked, "dp", split_axis=0, concat_axis=0, tiled=True)
    return gathered.reshape(grad_parts.shape[1:]), state[None, None]


def solution(mesh):
    return jax.shard_map(
        body,
        mesh=mesh,
        in_specs=(
            P("dp", "mp", "fsdp", None),
            P("mp", None),
            P("mp", "dp", "fsdp", None, None, None),
        ),
        out_specs=(P("mp", "fsdp", None), P("mp", "dp", "fsdp", None, None, None)),
        check_vma=False,
    )
```

```python
import numpy as np
import jax
import jax.numpy as jnp
from jax import lax
from jax.experimental import pallas as pl
from jax.experimental.pallas import tpu as pltpu
from jax.sharding import PartitionSpec as P

decay_rate = 0.95
epsilon = 1e-06
centre = 0.5


def root_coefficients():
    x = np.polynomial.Polynomial([centre, 1.0])
    t0 = (5.0 - x) / 4.0
    t1 = (5.0 - t0**4 * x) / 4.0
    return [float(c) for c in (t0 * t1).coef]


def dot(a, b, contract):
    return lax.dot_general(a, b, ((contract[:1], contract[1:]), ((), ())), preferred_element_type=jnp.float32)


def mean_square(x):
    return jnp.sum(jnp.sum(x * x, axis=0, keepdims=True), axis=1, keepdims=True) / x.size


def next_place(owners, seen, b):
    owner = owners[b]
    slot = seen[owner]
    seen[owner] = slot + 1
    return owner, slot


def place_kernel(owners_hbm, parts, out, owners, used, seen, total, sem):
    fetch = pltpu.make_async_copy(owners_hbm, owners, sem)
    fetch.start()
    replicas, count = parts.shape[:2]
    for b in range(count):
        row_sum = parts[0, b].astype(jnp.float32)
        for r in range(1, replicas):
            row_sum = row_sum + parts[r, b].astype(jnp.float32)
        total[b] = row_sum.astype(total.dtype)
    out[...] = jnp.zeros_like(out)
    for i in range(out.shape[0]):
        seen[i] = 0
    first = lax.axis_index("dp") * count
    fetch.wait()
    for b in range(count):
        owner, slot = next_place(owners, seen, first + b)
        out[owner, slot] = total[b]
    live = seen[lax.axis_index("fsdp")]
    for s in range(used.shape[0]):
        used[s : s + 1, :] = jnp.full((1, used.shape[1]), jnp.where(s < live, 1.0, 0.0), used.dtype)


def pick_kernel(owners, rows, out, seen):
    replicas, count = out.shape[:2]
    for i in range(rows.shape[0]):
        seen[i] = 0
    first = lax.axis_index("dp") * count
    for b in range(count):
        owner, slot = next_place(owners, seen, first + b)
        block = rows[owner, slot]
        for r in range(replicas):
            out[r, b] = block


def precondition_kernel(used, rows, factors, out, state):
    count, slots = rows.shape[:2]
    order = factors.shape[-1]
    r = root_coefficients()
    half_type = jnp.bfloat16
    diagonal = lax.broadcasted_iota(jnp.int32, (order, order), 0) == lax.broadcasted_iota(
        jnp.int32, (order, order), 1
    )
    wide = [rows[:, s].astype(jnp.float32).reshape(order, order) for s in range(slots)]
    g = [w.astype(half_type) for w in wide]
    pairs = [(s, side) for s in range(slots) for side in range(2)]
    factor = []
    for s, side in pairs:
        gram = dot(g[s], g[s], (1, 1) if side == 0 else (0, 0))
        factor.append(decay_rate * factors[s, side] + gram)
        state[s, side] = jnp.where(used[s : s + 1, :] > 0.0, factor[-1], factors[s, side])
    bound = [jnp.max(jnp.sum(jnp.abs(a), axis=0, keepdims=True), axis=1, keepdims=True) + epsilon for a in factor]
    m = [a * (1.0 / c) - jnp.where(diagonal, centre, 0.0) for a, c in zip(factor, bound)]
    mh = [x.astype(half_type) for x in m]
    m2 = [dot(x, x, (1, 0)) for x in mh]
    m2h = [x.astype(half_type) for x in m2]
    u = [(r[5] * x + r[6] * y).astype(half_type) for x, y in zip(m, m2)]
    w = [dot(x, y, (1, 0)) for x, y in zip(m2h, u)]
    v = [(r[3] * x + r[4] * y + z).astype(half_type) for x, y, z in zip(m, m2, w)]
    p = [dot(x, y, (1, 0)) for x, y in zip(m2h, v)]
    root = [
        (jnp.where(diagonal, r[0], 0.0) + r[1] * x + r[2] * y + z).astype(half_type) for x, y, z in zip(m, m2, p)
    ]
    half = [dot(root[2 * s], g[s], (1, 0)).astype(half_type) for s in range(slots)]
    raw = [dot(half[s], root[2 * s + 1], (1, 0)) for s in range(slots)]
    for s in range(slots):
        ratio = jnp.sqrt(mean_square(wide[s]) + epsilon) / jnp.sqrt(mean_square(raw[s]) + epsilon)
        out[:, s] = (raw[s] * ratio).reshape(count, rows.shape[2], order).astype(out.dtype)


def body(grad_parts, owner_ids, factors):
    fsdp_count = lax.axis_size("fsdp")
    replica_count = lax.axis_size("dp")
    slot_count = factors.shape[2]
    row_count, width = grad_parts.shape[2:]
    group_blocks = grad_parts.shape[1] // replica_count
    owners = owner_ids.reshape(-1)
    vmem = pl.BlockSpec(memory_space=pltpu.VMEM)
    smem = pl.BlockSpec(memory_space=pltpu.SMEM)
    seen = pltpu.SMEM((fsdp_count,), jnp.int32)
    params = pltpu.CompilerParams(vmem_limit_bytes=32 * 1024 * 1024)
    wire = jax.ShapeDtypeStruct((fsdp_count, slot_count, row_count, width), jnp.bfloat16)

    mine = grad_parts.reshape(replica_count, group_blocks, row_count, width)
    parts = lax.all_to_all(mine, "dp", split_axis=0, concat_axis=0, tiled=True)
    outgoing, known_owners, used = pl.pallas_call(
        place_kernel,
        out_shape=(
            wire,
            pltpu.SMEM(owners.shape, jnp.int32),
            pltpu.VMEM((slot_count, factors.shape[-1]), jnp.float32),
        ),
        in_specs=[pl.BlockSpec(memory_space=pltpu.HBM), vmem],
        out_specs=(vmem, smem, vmem),
        scratch_shapes=[
            seen,
            pltpu.VMEM(mine.shape[1:], jnp.bfloat16),
            pltpu.SemaphoreType.DMA,
        ],
        compiler_params=params,
        name="sum_and_place",
    )(pltpu.with_memory_space_constraint(owners, pltpu.HBM), parts)
    arrived = lax.all_to_all(outgoing, "fsdp", split_axis=0, concat_axis=0, tiled=True)
    directions, state = pl.pallas_call(
        precondition_kernel,
        out_shape=(wire, jax.ShapeDtypeStruct(factors.shape[2:], factors.dtype)),
        in_specs=[vmem, vmem, vmem],
        out_specs=(vmem, vmem),
        compiler_params=params,
        name="precondition",
    )(used, arrived, factors[0, 0])
    returned = lax.all_to_all(directions, "fsdp", split_axis=0, concat_axis=0, tiled=True)
    picked = pl.pallas_call(
        pick_kernel,
        out_shape=jax.ShapeDtypeStruct(mine.shape, jnp.bfloat16),
        in_specs=[smem, vmem],
        out_specs=vmem,
        scratch_shapes=[seen],
        compiler_params=params,
        name="pick",
    )(known_owners, returned)
    gathered = lax.all_to_all(picked, "dp", split_axis=0, concat_axis=0, tiled=True)
    return gathered.reshape(grad_parts.shape[1:]), state[None, None]


def solution(mesh):
    return jax.shard_map(
        body,
        mesh=mesh,
        in_specs=(
            P("dp", "mp", "fsdp", None),
            P("mp", None),
            P("mp", "dp", "fsdp", None, None, None),
        ),
        out_specs=(P("mp", "fsdp", None), P("mp", "dp", "fsdp", None, None, None)),
        check_vma=False,
    )
```
